32 devices in a mesh: segment: 4 (over y, x), dp: 8 (over z, core).
Axes of the slice: x: 2, y: 2, z: 4, core: 2. Of those that a mesh axis runs over, the one named last changes fastest.
Arguments:
- block_inputs: bfloat16 [4, 2, 24, 96, 768], P('segment', None, 'dp'), may hold values from -6 to 6
- top_grad: bfloat16 [2, 24, 96, 768], P(None, 'dp'), may hold values from -6 to 6
- depth_kernel: float32 [4, 7, 7, 768], P('segment'), may hold values from -0.875 to 0.875
- norm_gain: float32 [4, 768], P('segment'), may hold values from 0.5 to 2
- layer_scale: float32 [4, 768], P('segment'), may hold values from 0.3 to 1.5
- expand_weight: bfloat16 [4, 768, 3072], P('segment', 'dp'), may hold values from -0.21875 to 0.21875
- reduce_weight: bfloat16 [4, 3072, 768], P('segment', 'dp'), may hold values from -0.109375 to 0.109375
- chart_rows: int32 [2], replicated, may hold values from 6 to 24, as said below
Outputs:
- input_grads: bfloat16 [4, 2, 24, 96, 768], P('segment', None, 'dp')
- expand_grad: float32 [4, 768, 3072], P('segment', 'dp')
- reduce_grad: float32 [4, 3072, 768], P('segment', 'dp')
- kernel_grad: float32 [4, 7, 7, 768], P('segment')
- gain_grad: float32 [4, 768], P('segment')
- scale_grad: float32 [4, 768], P('segment')
The draws below stay inside these ranges and needn't reach their ends.
Inputs may be any that keep to these rules, and one draw needn't show every extreme that they name: `chart_rows`: rows are counted from the top of the chart; in every draw one chart fills all 24 rows.
All inputs are finite; a program needn't handle non-finite values.
Results may differ from the reference program's by a relative error of at most 0.018.
Values may be sent and summed in bfloat16 or wider, within the bound.
A program may use at most 128 MiB of HBM per device.

```python
import math
import jax
import jax.numpy as jnp
from jax import lax

C = 768
FF = 3072
KSIZE = 7
COLS = 96
MB = 2
ROWS_DEV = 3
IMG_ROWS = 24
SEGMENTS = 4
N_DP = 8


def draw_chart_rows(key, part):
    base = jax.random.randint(jax.random.fold_in(key, 21), (MB,), IMG_ROWS // 4, IMG_ROWS)
    order = jax.random.permutation(jax.random.fold_in(key, 22), MB)
    base = base.at[order[0]].set(IMG_ROWS)
    return base.astype(jnp.int32)


def block_scale(key, dims, split, least, top_value):
    factor_of = 1.0
    for position, shards_of in split:
        steps = jax.random.uniform(jax.random.fold_in(jax.random.fold_in(key, 6), position), (shards_of,), jnp.float32, least / len(split), top_value / len(split))
        factor_of = factor_of * jnp.repeat(jnp.exp(steps), dims[position] // shards_of).reshape((-1,) + (1,) * (len(dims) - 1 - position))
    return factor_of


def normal_values(own_key, extent, width, reach, shards=(), kind=jnp.bfloat16):
    loudness = block_scale(own_key, extent, shards, -0.22, 0.18) if shards else 1.0
    entries = jax.random.normal(own_key, extent, jnp.float32) * width * loudness
    return jnp.minimum(jnp.maximum(entries, -reach), reach).astype(kind)


def setup_inputs(seed: int = 0) -> dict:
    seeds = jax.random.split(jax.random.key(seed), 9)
    return {
        "block_inputs": normal_values(seeds[0], (SEGMENTS, MB, IMG_ROWS, COLS, C), 1.0, 6.0, ((0, 4), (2, 8))),
        "top_grad": normal_values(seeds[1], (MB, IMG_ROWS, COLS, C), 1.0, 6.0, ((1, 8),)),
        "depth_kernel": normal_values(seeds[2], (SEGMENTS, KSIZE, KSIZE, C), (KSIZE * KSIZE) ** -0.5, 0.875, ((0, 4),), jnp.float32),
        "norm_gain": jnp.clip(jnp.exp(math.log(2.0) - 1.3862944 * jax.random.uniform(seeds[3], (SEGMENTS, C), jnp.float32) ** block_scale(seeds[3], (SEGMENTS, C), ((0, 4),), -0.2, 0.2)), 0.5, 2.0),
        "layer_scale": jnp.clip(jnp.exp(math.log(1.5) - 1.60943787 * jax.random.uniform(seeds[4], (SEGMENTS, C), jnp.float32) ** block_scale(seeds[4], (SEGMENTS, C), ((0, 4),), -0.2, 0.2)), 0.3, 1.5),
        "expand_weight": normal_values(seeds[5], (SEGMENTS, C, FF), C ** -0.5, 0.21875, ((0, 4), (1, 8))),
        "reduce_weight": normal_values(seeds[6], (SEGMENTS, FF, C), FF ** -0.5, 0.109375, ((0, 4), (1, 8))),
        "chart_rows": draw_chart_rows(jax.random.fold_in(seeds[8], 71), 0),
    }


root_half = 0.7071067811865476
inv_root_tau = 0.3989422804014327
eps = 1e-06

def gelu_value(pre_act):
    return 0.5 * pre_act * (1.0 + lax.erf(pre_act * root_half))

def gelu_slope(pre_act):
    return 0.5 * (1.0 + lax.erf(pre_act * root_half)) + pre_act * jnp.exp(-0.5 * pre_act * pre_act) * inv_root_tau

def spread(padded, kernel, tile_rows, tile_cols):
    running = jnp.zeros(padded.shape[:-3] + (tile_rows, tile_cols, padded.shape[-1]), jnp.float32)
    for row_tap in range(kernel.shape[0]):
        for col_tap in range(kernel.shape[1]):
            running = running + kernel[row_tap, col_tap] * padded[..., row_tap:row_tap + tile_rows, col_tap:col_tap + tile_cols, :]
    return running

def kernel_terms(padded, grad_tile):
    tile_rows = grad_tile.shape[-3]
    tile_cols = grad_tile.shape[-2]
    axes_sum = tuple(range(grad_tile.ndim - 1))
    rows_out = []
    for row_tap in range(KSIZE):
        tap_line = []
        for col_tap in range(KSIZE):
            window = padded[..., row_tap:row_tap + tile_rows, col_tap:col_tap + tile_cols, :]
            tap_line.append(lax.optimization_barrier(jnp.sum(window * grad_tile, axis=axes_sum)))
        rows_out.append(jnp.stack(tap_line))
    return jnp.stack(rows_out)

def norm_stats(mixed):
    centred = mixed - lax.optimization_barrier(jnp.mean(mixed, axis=-1, keepdims=True))
    inv_sigma = lax.rsqrt(lax.optimization_barrier(jnp.mean(centred * centred, axis=-1, keepdims=True)) + eps)
    return (centred * inv_sigma, inv_sigma)

def shard_sums(former, latter):
    first_width = former.shape[-1]
    second_width = latter.shape[-1]
    former = former.reshape(MB, N_DP, ROWS_DEV * COLS, first_width).transpose(1, 0, 2, 3).reshape(N_DP, MB * ROWS_DEV * COLS, first_width)
    latter = latter.reshape(MB, N_DP, ROWS_DEV * COLS, second_width).transpose(1, 0, 2, 3).reshape(N_DP, MB * ROWS_DEV * COLS, second_width)

    def add_shard(running, pair_terms):
        shard_term = jnp.dot(pair_terms[0].T, pair_terms[1], preferred_element_type=jnp.float32)
        rounded = lax.optimization_barrier(shard_term.astype(jnp.bfloat16))
        return (running + rounded.astype(jnp.float32), None)
    running, _ = lax.scan(add_shard, jnp.zeros((first_width, second_width), jnp.float32), (former, latter))
    return running

def reference(block_inputs, top_grad, depth_kernel, norm_gain, layer_scale, expand_weight, reduce_weight, chart_rows):
    half_width = KSIZE // 2
    row_keep = (jnp.arange(IMG_ROWS, dtype=jnp.int32)[None, :] < chart_rows[:, None]).astype(jnp.float32)[:, :, None, None]
    grad_norm = 1.0 / math.sqrt(MB * IMG_ROWS * COLS)
    pads = ((0, 0), (half_width, half_width), (half_width, half_width), (0, 0))
    arriving = top_grad
    grads_in, grads_expand, grads_reduce, grads_kernel, grads_gain, grads_scale = ([], [], [], [], [], [])
    for segment_index in range(SEGMENTS - 1, -1, -1):
        kernel = depth_kernel[segment_index]
        gain_row = norm_gain[segment_index]
        scale_row = layer_scale[segment_index]
        masked = block_inputs[segment_index].astype(jnp.float32) * row_keep
        padded = jnp.pad(masked, pads)
        mixed = spread(padded, kernel, IMG_ROWS, COLS)
        normal_z, inv_sigma = norm_stats(mixed)
        normed = (normal_z * gain_row).astype(jnp.bfloat16).reshape(-1, C)
        pre_act = jnp.dot(normed, expand_weight[segment_index], preferred_element_type=jnp.float32)
        hidden = gelu_value(pre_act).astype(jnp.bfloat16)
        out_grad = (arriving.astype(jnp.float32) * row_keep).astype(jnp.bfloat16).reshape(-1, C)
        scaled_grad = (out_grad.astype(jnp.float32) * scale_row).astype(jnp.bfloat16)
        hidden_grad = jnp.dot(scaled_grad, reduce_weight[segment_index].T, preferred_element_type=jnp.float32)
        pre_grad = (hidden_grad * gelu_slope(pre_act)).astype(jnp.bfloat16)
        normed_grad = jnp.dot(pre_grad, expand_weight[segment_index].T, preferred_element_type=jnp.float32).reshape(MB, IMG_ROWS, COLS, C)
        scaled_u = normed_grad * gain_row
        mixed_grad = inv_sigma * (scaled_u - lax.optimization_barrier(jnp.mean(scaled_u, axis=-1, keepdims=True)) - normal_z * lax.optimization_barrier(jnp.mean(scaled_u * normal_z, axis=-1, keepdims=True)))
        mixed_grad = lax.optimization_barrier(mixed_grad.astype(jnp.bfloat16)).astype(jnp.float32)
        spread_back = spread(jnp.pad(mixed_grad, pads), kernel[::-1, ::-1], IMG_ROWS, COLS)
        input_grad = (arriving.astype(jnp.float32) + row_keep * spread_back).astype(jnp.bfloat16)
        hidden_sum = shard_sums(hidden.reshape(MB, IMG_ROWS, COLS, FF), out_grad.reshape(MB, IMG_ROWS, COLS, C))
        input_sum = shard_sums(normed.reshape(MB, IMG_ROWS, COLS, C), pre_grad.reshape(MB, IMG_ROWS, COLS, FF))
        grads_in.append(input_grad)
        grads_reduce.append(hidden_sum * scale_row * grad_norm)
        grads_expand.append(input_sum * grad_norm)
        grads_scale.append(lax.optimization_barrier(jnp.sum(reduce_weight[segment_index].astype(jnp.float32) * hidden_sum, axis=0)) * grad_norm)
        grads_kernel.append(kernel_terms(padded, mixed_grad) * grad_norm)
        grads_gain.append(lax.optimization_barrier(jnp.sum(normed_grad * normal_z, axis=(0, 1, 2))) * grad_norm)
        arriving = input_grad
    return (jnp.stack(grads_in[::-1]), jnp.stack(grads_expand[::-1]), jnp.stack(grads_reduce[::-1]), jnp.stack(grads_kernel[::-1]), jnp.stack(grads_gain[::-1]), jnp.stack(grads_scale[::-1]))
```

```python
import math

import jax
import jax.numpy as jnp
from jax import lax
from jax.experimental import pallas as pl
from jax.sharding import PartitionSpec as P

KSIZE = 7


root_half = 0.7071067811865476
inv_root_tau = 0.3989422804014327
eps = 1e-06


def extended(block, sides, width):
    for axis, dim in sides:
        count = lax.axis_size(axis)
        forward = [(i, i + 1) for i in range(count - 1)]
        backward = [(target, source) for source, target in forward]
        low = lax.ppermute(
            lax.slice_in_dim(block, block.shape[dim] - width, None, axis=dim), axis, forward
        )
        high = lax.ppermute(lax.slice_in_dim(block, 0, width, axis=dim), axis, backward)
        block = jnp.concatenate([low, block, high], axis=dim)
    return block


def from_behind(value, axis, by):
    length = lax.axis_size(axis)
    pairs = [(i, i + by) for i in range(length) if 0 <= i + by < length]
    return lax.ppermute(value, axis, pairs)


def gelu_value(pre_act):
    return 0.5 * pre_act * (1.0 + lax.erf(pre_act * root_half))


def gelu_slope(pre_act):
    return (
        0.5 * (1.0 + lax.erf(pre_act * root_half))
        + pre_act * jnp.exp(-0.5 * pre_act * pre_act) * inv_root_tau
    )


def spread(padded, kernel, tile_rows, tile_cols):
    running = jnp.zeros(padded.shape[:-3] + (tile_rows, tile_cols, padded.shape[-1]), jnp.float32)
    for row_tap in range(kernel.shape[0]):
        for col_tap in range(kernel.shape[1]):
            running = (
                running
                + kernel[row_tap, col_tap]
                * padded[..., row_tap : row_tap + tile_rows, col_tap : col_tap + tile_cols, :]
            )
    return running


LANES = 128


def spread_kernel(x_ref, k_ref, o_ref):
    tile_rows, tile_cols = o_ref.shape[:2]
    sums = [None] * tile_rows
    for line in range(tile_rows + KSIZE - 1):
        for col_tap in range(KSIZE):
            window = x_ref[line, col_tap : col_tap + tile_cols, :].astype(jnp.float32)
            for row in range(tile_rows):
                row_tap = line - row
                if 0 <= row_tap < KSIZE:
                    tap = row_tap * KSIZE + col_tap
                    term = k_ref[tap : tap + 1, :] * window
                    sums[row] = term if sums[row] is None else sums[row] + term
    for row in range(tile_rows):
        o_ref[row] = sums[row]


def spread_tile(padded, kernel, tile_rows, tile_cols):
    rows, cols, channels = padded.shape
    return pl.pallas_call(
        spread_kernel,
        grid=(channels // LANES,),
        in_specs=[
            pl.BlockSpec((rows, cols, LANES), lambda i: (0, 0, i)),
            pl.BlockSpec((KSIZE * KSIZE, LANES), lambda i: (0, i)),
        ],
        out_specs=pl.BlockSpec((tile_rows, tile_cols, LANES), lambda i: (0, 0, i)),
        out_shape=jax.ShapeDtypeStruct((tile_rows, tile_cols, channels), jnp.float32),
        cost_estimate=pl.CostEstimate(
            flops=8 * KSIZE * KSIZE * tile_rows * tile_cols * channels,
            bytes_accessed=4 * rows * cols * channels,
            transcendentals=0,
        ),
    )(padded.astype(jnp.float32), kernel.reshape(-1, channels))


def sums_kernel(x_ref, g_ref, o_ref):
    micro_count, tile_rows, tile_cols = g_ref.shape[:3]
    for row_tap in range(KSIZE):
        for col_tap in range(KSIZE):
            folded = None
            for chart in range(micro_count):
                for row in range(tile_rows):
                    window = x_ref[chart, row + row_tap, col_tap : col_tap + tile_cols, :]
                    term = window * g_ref[chart, row]
                    folded = term if folded is None else folded + term
            tap = row_tap * KSIZE + col_tap
            o_ref[tap : tap + 1, :] = jnp.sum(folded, axis=0, keepdims=True)


def kernel_sums(padded, grads):
    micro_count, rows, cols, channels = padded.shape
    tile_rows, tile_cols = grads.shape[1:3]
    return pl.pallas_call(
        sums_kernel,
        grid=(channels // LANES,),
        in_specs=[
            pl.BlockSpec((micro_count, rows, cols, LANES), lambda i: (0, 0, 0, i)),
            pl.BlockSpec((micro_count, tile_rows, tile_cols, LANES), lambda i: (0, 0, 0, i)),
        ],
        out_specs=pl.BlockSpec((KSIZE * KSIZE, LANES), lambda i: (0, i)),
        out_shape=jax.ShapeDtypeStruct((KSIZE * KSIZE, channels), jnp.float32),
        cost_estimate=pl.CostEstimate(
            flops=8 * KSIZE * KSIZE * micro_count * tile_rows * tile_cols * channels,
            bytes_accessed=4 * micro_count * rows * cols * channels,
            transcendentals=0,
        ),
    )(padded.astype(jnp.float32), grads.astype(jnp.float32))


def norm_stats(mixed):
    centred = mixed - jnp.mean(mixed, axis=-1, keepdims=True)
    inv_sigma = lax.rsqrt(jnp.mean(centred * centred, axis=-1, keepdims=True) + eps)
    return (centred * inv_sigma, inv_sigma)


def contract_rows(former, latter):
    return lax.dot_general(
        former, latter, (((0,), (0,)), ((), ())), preferred_element_type=jnp.float32
    )


def contract_cols(former, latter):
    return lax.dot_general(
        former, latter, (((1,), (1,)), ((), ())), preferred_element_type=jnp.float32
    )


def across_groups(count):
    return [[core + 2 * k for k in range(count // 2)] for core in range(2)]


def swap_cores(value):
    count = lax.axis_size("dp")
    pairs = [(i, i + 1 - 2 * (i % 2)) for i in range(count)]
    return lax.ppermute(value, "dp", pairs)


def gather_chips(shard):
    return lax.all_gather(
        shard, "dp", axis=0, axis_index_groups=across_groups(lax.axis_size("dp"))
    )


def gather_cores(part):
    other = swap_cores(part)
    first = lax.rem(lax.axis_index("dp"), 2) == 0
    low = jnp.where(first, part, other)
    high = jnp.where(first, other, part)
    return jnp.stack([low, high], axis=1).reshape(-1, part.shape[-1])


def scatter_cores(total):
    count = lax.axis_size("dp")
    split = total.reshape(count // 2, 2, total.shape[0] // count, total.shape[1])
    core = lax.rem(lax.axis_index("dp"), 2)
    away = lax.dynamic_index_in_dim(split, 1 - core, 1, keepdims=False).astype(jnp.bfloat16)
    mine = lax.dynamic_index_in_dim(split, core, 1, keepdims=False)
    return (mine + swap_cores(away).astype(jnp.float32)).astype(jnp.bfloat16)


def scatter_chips(pair_sum):
    return lax.psum_scatter(
        pair_sum,
        "dp",
        scatter_dimension=0,
        axis_index_groups=across_groups(lax.axis_size("dp")),
    ).astype(jnp.float32)


def per_device(
    block_inputs,
    top_grad,
    depth_kernel,
    norm_gain,
    layer_scale,
    expand_weight,
    reduce_weight,
    chart_rows,
):
    segment_count = lax.axis_size("segment")
    group_count = lax.axis_size("dp")
    segment_index = lax.axis_index("segment")
    group_index = lax.axis_index("dp")
    micro_count, tile_rows, tile_cols, channels = block_inputs.shape[1:]
    hidden_width = expand_weight.shape[2]
    half_width = KSIZE // 2
    tokens = tile_rows * tile_cols
    kernel = depth_kernel[0]
    flipped = kernel[::-1, ::-1]
    gain_row = norm_gain[0]
    scale_row = layer_scale[0]
    row_ids = group_index * tile_rows + jnp.arange(tile_rows, dtype=jnp.int32)
    row_keep = (row_ids[None, :] < chart_rows[:, None]).astype(jnp.float32)
    expand_part = gather_chips(expand_weight[0])
    masked = (block_inputs[0].astype(jnp.float32) * row_keep[:, :, None, None]).astype(jnp.bfloat16)
    rimmed = extended(masked, (("dp", 1),), half_width)
    rimmed = jnp.pad(rimmed, ((0, 0), (0, 0), (half_width, half_width), (0, 0)))
    reduce_part = gather_chips(reduce_weight[0])
    expand_full = gather_cores(expand_part)

    mixed = spread(rimmed.astype(jnp.float32), kernel, tile_rows, tile_cols)
    normal_z, inv_sigma = norm_stats(mixed.reshape(micro_count, tokens, channels))
    normed = (normal_z * gain_row).astype(jnp.bfloat16).reshape(-1, channels)
    pre_act = jnp.dot(normed, expand_full, preferred_element_type=jnp.float32)
    hidden = gelu_value(pre_act).astype(jnp.bfloat16)
    slope = gelu_slope(pre_act).reshape(micro_count, tokens, hidden_width)
    reduce_full = gather_cores(reduce_part)

    def pick(array, slot):
        return lax.dynamic_index_in_dim(array, slot, 0, keepdims=False)

    def put(array, value, slot):
        return lax.dynamic_update_index_in_dim(array, value, slot, 0)

    incoming = jnp.zeros((tokens, channels), jnp.bfloat16)
    tops = top_grad.reshape(micro_count, tokens, channels)
    token_keep = jnp.repeat(row_keep, tile_cols, axis=1)[:, :, None]
    out_grads = jnp.zeros((micro_count, tokens, channels), jnp.bfloat16)
    pre_grads = jnp.zeros((micro_count, tokens, hidden_width), jnp.bfloat16)
    mixed_grads = jnp.zeros((micro_count, tokens, channels), jnp.bfloat16)
    normed_grads = jnp.zeros((micro_count, tokens, channels), jnp.float32)
    results = jnp.zeros((micro_count, tokens, channels), jnp.bfloat16)
    ticks = segment_count + micro_count - 1
    for tick_id in range(ticks):
        slot = jnp.clip(tick_id - (segment_count - 1 - segment_index), 0, micro_count - 1)
        arriving = jnp.where(segment_index == segment_count - 1, pick(tops, slot), incoming)
        keep = pick(token_keep, slot)
        out_grad = (arriving.astype(jnp.float32) * keep).astype(jnp.bfloat16)
        out_grads = put(out_grads, out_grad, slot)
        if tick_id == ticks - 1:
            flat_out = out_grads.reshape(-1, channels)
            hidden_pair = scatter_cores(contract_rows(hidden, flat_out))
        scaled_grad = (out_grad.astype(jnp.float32) * scale_row).astype(jnp.bfloat16)
        hidden_grad = contract_cols(scaled_grad, reduce_full)
        pre_grad = (hidden_grad * pick(slope, slot)).astype(jnp.bfloat16)
        pre_grads = put(pre_grads, pre_grad, slot)
        if tick_id == ticks - 1:
            hidden_sum = scatter_chips(hidden_pair)
            input_pair = scatter_cores(
                contract_rows(normed, pre_grads.reshape(-1, hidden_width))
            )
        normed_grad = contract_cols(pre_grad, expand_full)
        normed_grads = put(normed_grads, normed_grad, slot)
        zed = pick(normal_z, slot)
        scaled_u = normed_grad * gain_row
        mixed_grad = (
            pick(inv_sigma, slot)
            * (
                scaled_u
                - jnp.mean(scaled_u, axis=-1, keepdims=True)
                - zed * jnp.mean(scaled_u * zed, axis=-1, keepdims=True)
            )
        ).astype(jnp.bfloat16)
        mixed_grads = put(mixed_grads, mixed_grad, slot)
        if tick_id == ticks - 1:
            input_sum = scatter_chips(input_pair)
        mixed_tile = mixed_grad.reshape(tile_rows, tile_cols, channels)
        grad_rimmed = extended(mixed_tile, (("dp", 0),), half_width)
        grad_padded = jnp.pad(grad_rimmed, ((0, 0), (half_width, half_width), (0, 0)))
        spread_back = spread_tile(grad_padded, flipped, tile_rows, tile_cols)
        input_grad = (
            arriving.astype(jnp.float32) + keep * spread_back.reshape(tokens, channels)
        ).astype(jnp.bfloat16)
        results = put(results, input_grad, slot)
        if tick_id < ticks - 1:
            incoming = from_behind(input_grad, "segment", -1)
    kernel_part = kernel_sums(
        rimmed, mixed_grads.reshape(micro_count, tile_rows, tile_cols, channels)
    )
    gain_part = jnp.sum(normed_grads * normal_z, axis=(0, 1))
    branch = jnp.dot(hidden, reduce_full, preferred_element_type=jnp.float32)
    scale_part = jnp.sum(flat_out.astype(jnp.float32) * branch, axis=0)
    small = jnp.concatenate([kernel_part, gain_part[None], scale_part[None]], axis=0)
    small = lax.psum(small, "dp")
    taps = KSIZE * KSIZE
    grad_norm = 1.0 / math.sqrt(micro_count * tokens * group_count)
    small = small * grad_norm
    return (
        results.reshape((1,) + block_inputs.shape[1:]),
        (input_sum * grad_norm)[None],
        (hidden_sum * scale_row * grad_norm)[None],
        small[:taps].reshape(1, KSIZE, KSIZE, channels),
        small[taps][None],
        small[taps + 1][None],
    )


def solution(mesh):
    placed = (
        P("segment", None, "dp", None, None),
        P(None, "dp", None, None),
        P("segment", None, None, None),
        P("segment", None),
        P("segment", None),
        P("segment", "dp", None),
        P("segment", "dp", None),
        P(),
    )
    return jax.shard_map(
        per_device,
        mesh=mesh,
        in_specs=placed,
        out_specs=(
            P("segment", None, "dp", None, None),
            P("segment", "dp", None),
            P("segment", "dp", None),
            P("segment", None, None, None),
            P("segment", None),
            P("segment", None),
        ),
        check_vma=False,
    )
```

```python
import math

import jax
import jax.numpy as jnp
from jax import lax
from jax.experimental import pallas as pl
from jax.sharding import PartitionSpec as P

KSIZE = 7


root_half = 0.7071067811865476
inv_root_tau = 0.3989422804014327
eps = 1e-06


def extended(block, sides, width):
    for axis, dim in sides:
        count = lax.axis_size(axis)
        forward = [(i, i + 1) for i in range(count - 1)]
        backward = [(target, source) for source, target in forward]
        low = lax.ppermute(
            lax.slice_in_dim(block, block.shape[dim] - width, None, axis=dim), axis, forward
        )
        high = lax.ppermute(lax.slice_in_dim(block, 0, width, axis=dim), axis, backward)
        block = jnp.concatenate([low, block, high], axis=dim)
    return block


def from_behind(value, axis, by):
    length = lax.axis_size(axis)
    pairs = [(i, i + by) for i in range(length) if 0 <= i + by < length]
    return lax.ppermute(value, axis, pairs)


def gelu_value(pre_act):
    return 0.5 * pre_act * (1.0 + lax.erf(pre_act * root_half))


def gelu_slope(pre_act):
    return (
        0.5 * (1.0 + lax.erf(pre_act * root_half))
        + pre_act * jnp.exp(-0.5 * pre_act * pre_act) * inv_root_tau
    )


LANES = 128


def spread_kernel(x_ref, k_ref, *rest):
    o_ref = rest[-1]
    tile_rows, tile_cols = o_ref.shape[:2]
    sums = [None] * tile_rows
    for line in range(tile_rows + KSIZE - 1):
        for col_tap in range(KSIZE):
            window = x_ref[line, col_tap : col_tap + tile_cols, :]
            for row in range(tile_rows):
                row_tap = line - row
                if 0 <= row_tap < KSIZE:
                    tap = row_tap * KSIZE + col_tap
                    term = k_ref[tap : tap + 1, :] * window
                    sums[row] = term if sums[row] is None else sums[row] + term
    for row in range(tile_rows):
        if len(rest) > 1:
            held = rest[0][row].astype(jnp.float32) + rest[1][row : row + 1, :] * sums[row]
            o_ref[row] = held.astype(jnp.bfloat16)
        else:
            o_ref[row] = sums[row]


def spread_tile(padded, taps, *extra):
    rows, cols, channels = padded.shape
    tile_rows, tile_cols = rows - KSIZE + 1, cols - KSIZE + 1
    tile = pl.BlockSpec((tile_rows, tile_cols, LANES), lambda i: (0, 0, i))
    more = [tile, pl.BlockSpec((tile_rows, LANES), lambda i: (0, 0))] if extra else []
    return pl.pallas_call(
        spread_kernel,
        grid=(channels // LANES,),
        in_specs=[
            pl.BlockSpec((rows, cols, LANES), lambda i: (0, 0, i)),
            pl.BlockSpec((KSIZE * KSIZE, LANES), lambda i: (0, i)),
        ]
        + more,
        out_specs=tile,
        out_shape=jax.ShapeDtypeStruct(
            (tile_rows, tile_cols, channels), jnp.bfloat16 if extra else jnp.float32
        ),
        cost_estimate=pl.CostEstimate(
            flops=8 * KSIZE * KSIZE * tile_rows * tile_cols * channels,
            bytes_accessed=4 * rows * cols * channels,
            transcendentals=0,
        ),
    )(padded.astype(jnp.float32), taps, *extra)


def sums_kernel(x_ref, g_ref, o_ref):
    micro_count, tile_rows, tile_cols = g_ref.shape[:3]
    for row_tap in range(KSIZE):
        for col_tap in range(KSIZE):
            folded = None
            for chart in range(micro_count):
                for row in range(tile_rows):
                    window = x_ref[chart, row + row_tap, col_tap : col_tap + tile_cols, :]
                    term = window * g_ref[chart, row]
                    folded = term if folded is None else folded + term
            tap = row_tap * KSIZE + col_tap
            o_ref[tap : tap + 1, :] = jnp.sum(folded, axis=0, keepdims=True)


def kernel_sums(padded, grads):
    micro_count, rows, cols, channels = padded.shape
    tile_rows, tile_cols = grads.shape[1:3]
    return pl.pallas_call(
        sums_kernel,
        grid=(channels // LANES,),
        in_specs=[
            pl.BlockSpec((micro_count, rows, cols, LANES), lambda i: (0, 0, 0, i)),
            pl.BlockSpec((micro_count, tile_rows, tile_cols, LANES), lambda i: (0, 0, 0, i)),
        ],
        out_specs=pl.BlockSpec((KSIZE * KSIZE, LANES), lambda i: (0, i)),
        out_shape=jax.ShapeDtypeStruct((KSIZE * KSIZE, channels), jnp.float32),
        cost_estimate=pl.CostEstimate(
            flops=8 * KSIZE * KSIZE * micro_count * tile_rows * tile_cols * channels,
            bytes_accessed=4 * micro_count * rows * cols * channels,
            transcendentals=0,
        ),
    )(padded.astype(jnp.float32), grads.astype(jnp.float32))


def norm_stats(mixed):
    centred = mixed - jnp.mean(mixed, axis=-1, keepdims=True)
    inv_sigma = lax.rsqrt(jnp.mean(centred * centred, axis=-1, keepdims=True) + eps)
    return (centred * inv_sigma, inv_sigma)


def contract_rows(former, latter):
    return lax.dot_general(
        former, latter, (((0,), (0,)), ((), ())), preferred_element_type=jnp.float32
    )


def contract_cols(former, latter):
    return lax.dot_general(
        former, latter, (((1,), (1,)), ((), ())), preferred_element_type=jnp.float32
    )


def chip_pairs(low, high, step):
    return [(2 * z + core, 2 * (z + step) + core) for z in range(low, high) for core in range(2)]


def swap_cores(value):
    count = lax.axis_size("dp")
    pairs = [(i, i + 1 - 2 * (i % 2)) for i in range(count)]
    return lax.ppermute(value, "dp", pairs)


def gather_step(right, left, hop):
    chips = lax.axis_size("dp") // 2
    return (
        lax.ppermute(right, "dp", chip_pairs(hop - 1, chips - 1, 1)),
        lax.ppermute(left, "dp", chip_pairs(1, chips - hop + 1, -1)),
    )


def gather_join(shard, hops):
    chips = lax.axis_size("dp") // 2
    line = [right for right, _ in hops[::-1]] + [shard] + [left for _, left in hops]
    place = lax.axis_index("dp") // 2
    return lax.dynamic_slice_in_dim(jnp.stack(line), chips - 1 - place, chips, 0)


def gather_two(first, second):
    chips = lax.axis_size("dp") // 2
    early, late = [], []
    for hop in range(1, chips + 1):
        if hop > 1:
            ahead = late[-1] if late else (second, second)
            if hop == 2:
                second = lax.optimization_barrier((second,) + early[0])[0]
                ahead = (second, second)
            late.append(gather_step(*ahead, hop - 1))
        if hop < chips:
            early.append(gather_step(*(early[-1] if early else (first, first)), hop))
    return gather_join(first, early), gather_join(second, late)


def gather_cores(part):
    other = swap_cores(part)
    first = lax.rem(lax.axis_index("dp"), 2) == 0
    low = jnp.where(first, part, other)
    high = jnp.where(first, other, part)
    return jnp.stack([low, high], axis=1).reshape(-1, part.shape[-1])


def scatter_cores(total):
    count = lax.axis_size("dp")
    split = total.astype(jnp.bfloat16)
    split = split.reshape(count // 2, 2, total.shape[0] // count, total.shape[1])
    core = lax.rem(lax.axis_index("dp"), 2)
    away = lax.dynamic_index_in_dim(split, 1 - core, 1, keepdims=False)
    mine = lax.dynamic_index_in_dim(split, core, 1, keepdims=False)
    both = mine.astype(jnp.float32) + swap_cores(away).astype(jnp.float32)
    return both.astype(jnp.bfloat16)


def scatter_chips(pair_sum):
    chips = pair_sum.shape[0]
    place = lax.axis_index("dp") // 2

    def term(index, held):
        block = lax.dynamic_index_in_dim(
            pair_sum, jnp.clip(index, 0, chips - 1), 0, keepdims=False
        )
        return block if held is None else sum_two(block, held).astype(jnp.bfloat16)

    right, left = None, None
    for hop in range(1, chips):
        away = chips - hop
        right = lax.ppermute(
            term(place + away, right), "dp", chip_pairs(0, min(hop, chips - 1), 1)
        )
        left = lax.ppermute(term(place - away, left), "dp", chip_pairs(max(away, 1), chips, -1))
    total = sum_two(term(place, None), right)
    return total if left is None else sum_two(total, left)


def sum_two(former, latter):
    return former.astype(jnp.float32) + latter.astype(jnp.float32)


def sum_small(value):
    count = lax.axis_size("dp")
    if count & (count - 1):
        return lax.psum(value, "dp")
    reach = 1
    while reach < count:
        pairs = [(i, i ^ reach) for i in range(count)]
        value = value + lax.ppermute(value, "dp", pairs)
        reach *= 2
    return value


def per_device(
    block_inputs,
    top_grad,
    depth_kernel,
    norm_gain,
    layer_scale,
    expand_weight,
    reduce_weight,
    chart_rows,
):
    segment_count = lax.axis_size("segment")
    group_count = lax.axis_size("dp")
    segment_index = lax.axis_index("segment")
    group_index = lax.axis_index("dp")
    micro_count, tile_rows, tile_cols, channels = block_inputs.shape[1:]
    hidden_width = expand_weight.shape[2]
    half_width = KSIZE // 2
    tokens = tile_rows * tile_cols
    kernel = depth_kernel[0]
    flipped = kernel[::-1, ::-1]
    gain_row = norm_gain[0]
    scale_row = layer_scale[0]
    row_ids = group_index * tile_rows + jnp.arange(tile_rows, dtype=jnp.int32)
    row_keep = (row_ids[None, :] < chart_rows[:, None]).astype(jnp.float32)
    masked = (block_inputs[0].astype(jnp.float32) * row_keep[:, :, None, None]).astype(jnp.bfloat16)
    rimmed = extended(masked, (("dp", 1),), half_width)
    rimmed = jnp.pad(rimmed, ((0, 0), (0, 0), (half_width, half_width), (0, 0)))
    expand_part, reduce_part = gather_two(expand_weight[0], reduce_weight[0])
    expand_full = gather_cores(expand_part)

    taps_forward = kernel.reshape(-1, channels)
    taps_back = flipped.reshape(-1, channels)
    mixed = jnp.stack([spread_tile(rimmed[m], taps_forward) for m in range(micro_count)])
    normal_z, inv_sigma = norm_stats(mixed.reshape(micro_count, tokens, channels))
    normed = (normal_z * gain_row).astype(jnp.bfloat16).reshape(-1, channels)
    pre_act = jnp.dot(normed, expand_full, preferred_element_type=jnp.float32)
    hidden = gelu_value(pre_act).astype(jnp.bfloat16)
    slope = gelu_slope(pre_act).reshape(micro_count, tokens, hidden_width)
    reduce_full = gather_cores(reduce_part)

    def pick(array, slot):
        return lax.dynamic_index_in_dim(array, slot, 0, keepdims=False)

    def put(array, value, slot):
        return lax.dynamic_update_index_in_dim(array, value, slot, 0)

    incoming = jnp.zeros((tokens, channels), jnp.bfloat16)
    tops = top_grad.reshape(micro_count, tokens, channels)
    token_keep = jnp.repeat(row_keep, tile_cols, axis=1)[:, :, None]
    out_grads = jnp.zeros((micro_count, tokens, channels), jnp.bfloat16)
    pre_grads = jnp.zeros((micro_count, tokens, hidden_width), jnp.bfloat16)
    mixed_grads = jnp.zeros((micro_count, tokens, channels), jnp.bfloat16)
    normed_grads = jnp.zeros((micro_count, tokens, channels), jnp.float32)
    results = jnp.zeros((micro_count, tokens, channels), jnp.bfloat16)
    ticks = segment_count + micro_count - 1
    for tick_id in range(ticks):
        slot = jnp.clip(tick_id - (segment_count - 1 - segment_index), 0, micro_count - 1)
        arriving = jnp.where(segment_index == segment_count - 1, pick(tops, slot), incoming)
        keep = pick(token_keep, slot)
        out_grad = (arriving.astype(jnp.float32) * keep).astype(jnp.bfloat16)
        out_grads = put(out_grads, out_grad, slot)
        if tick_id == ticks - 1:
            flat_out = out_grads.reshape(-1, channels)
            hidden_pair = scatter_cores(contract_rows(hidden, flat_out))
        scaled_grad = (out_grad.astype(jnp.float32) * scale_row).astype(jnp.bfloat16)
        hidden_grad = contract_cols(scaled_grad, reduce_full)
        pre_grad = (hidden_grad * pick(slope, slot)).astype(jnp.bfloat16)
        pre_grads = put(pre_grads, pre_grad, slot)
        if tick_id == ticks - 1:
            hidden_sum = scatter_chips(hidden_pair)
            input_pair = scatter_cores(
                contract_rows(normed, pre_grads.reshape(-1, hidden_width))
            )
        normed_grad = contract_cols(pre_grad, expand_full)
        normed_grads = put(normed_grads, normed_grad, slot)
        zed = pick(normal_z, slot)
        scaled_u = normed_grad * gain_row
        mixed_grad = (
            pick(inv_sigma, slot)
            * (
                scaled_u
                - jnp.mean(scaled_u, axis=-1, keepdims=True)
                - zed * jnp.mean(scaled_u * zed, axis=-1, keepdims=True)
            )
        ).astype(jnp.bfloat16)
        mixed_grads = put(mixed_grads, mixed_grad, slot)
        if tick_id == ticks - 1:
            input_sum = scatter_chips(input_pair)
        mixed_tile = mixed_grad.reshape(tile_rows, tile_cols, channels)
        grad_rimmed = extended(mixed_tile, (("dp", 0),), half_width)
        grad_padded = jnp.pad(grad_rimmed, ((0, 0), (half_width, half_width), (0, 0)))
        line_keep = jnp.broadcast_to(pick(row_keep, slot)[:, None], (tile_rows, LANES))
        input_grad = spread_tile(
            grad_padded, taps_back, arriving.reshape(tile_rows, tile_cols, channels), line_keep
        ).reshape(tokens, channels)
        results = put(results, input_grad, slot)
        if tick_id < ticks - 1:
            incoming = from_behind(input_grad, "segment", -1)
    kernel_part = kernel_sums(
        rimmed, mixed_grads.reshape(micro_count, tile_rows, tile_cols, channels)
    )
    gain_part = jnp.sum(normed_grads * normal_z, axis=(0, 1))
    branch = jnp.dot(hidden, reduce_full, preferred_element_type=jnp.float32)
    scale_part = jnp.sum(flat_out.astype(jnp.float32) * branch, axis=0)
    small = jnp.concatenate([kernel_part, gain_part[None], scale_part[None]], axis=0)
    small = sum_small(small)
    taps = KSIZE * KSIZE
    grad_norm = 1.0 / math.sqrt(micro_count * tokens * group_count)
    small = small * grad_norm
    return (
        results.reshape((1,) + block_inputs.shape[1:]),
        (input_sum * grad_norm)[None],
        (hidden_sum * scale_row * grad_norm)[None],
        small[:taps].reshape(1, KSIZE, KSIZE, channels),
        small[taps][None],
        small[taps + 1][None],
    )


def solution(mesh):
    placed = (
        P("segment", None, "dp", None, None),
        P(None, "dp", None, None),
        P("segment", None, None, None),
        P("segment", None),
        P("segment", None),
        P("segment", "dp", None),
        P("segment", "dp", None),
        P(),
    )
    return jax.shard_map(
        per_device,
        mesh=mesh,
        in_specs=placed,
        out_specs=(
            P("segment", None, "dp", None, None),
            P("segment", "dp", None),
            P("segment", "dp", None),
            P("segment", None, None, None),
            P("segment", None),
            P("segment", None),
        ),
        check_vma=False,
    )
```

```python
import math

import jax
import jax.numpy as jnp
from jax import lax
from jax.experimental import pallas as pl
from jax.sharding import PartitionSpec as P

KSIZE = 7


root_half = 0.7071067811865476
inv_root_tau = 0.3989422804014327
eps = 1e-06


def extended(block, sides, width):
    for axis, dim in sides:
        count = lax.axis_size(axis)
        forward = [(i, i + 1) for i in range(count - 1)]
        backward = [(target, source) for source, target in forward]
        low = lax.ppermute(
            lax.slice_in_dim(block, block.shape[dim] - width, None, axis=dim), axis, forward
        )
        high = lax.ppermute(lax.slice_in_dim(block, 0, width, axis=dim), axis, backward)
        block = jnp.concatenate([low, block, high], axis=dim)
    return block


def from_behind(value, axis, by):
    length = lax.axis_size(axis)
    pairs = [(i, i + by) for i in range(length) if 0 <= i + by < length]
    return lax.ppermute(value, axis, pairs)


def gelu_value(pre_act):
    return 0.5 * pre_act * (1.0 + lax.erf(pre_act * root_half))


def gelu_slope(pre_act):
    return (
        0.5 * (1.0 + lax.erf(pre_act * root_half))
        + pre_act * jnp.exp(-0.5 * pre_act * pre_act) * inv_root_tau
    )


LANES = 128


def spread_kernel(x_ref, k_ref, *rest):
    o_ref = rest[-1]
    tile_rows, tile_cols = o_ref.shape[:2]
    sums = [None] * tile_rows
    for line in range(tile_rows + KSIZE - 1):
        for col_tap in range(KSIZE):
            window = x_ref[line, col_tap : col_tap + tile_cols, :]
            for row in range(tile_rows):
                row_tap = line - row
                if 0 <= row_tap < KSIZE:
                    tap = row_tap * KSIZE + col_tap
                    term = k_ref[tap : tap + 1, :] * window
                    sums[row] = term if sums[row] is None else sums[row] + term
    for row in range(tile_rows):
        if len(rest) > 1:
            held = rest[0][row].astype(jnp.float32) + rest[1][row : row + 1, :] * sums[row]
            o_ref[row] = held.astype(jnp.bfloat16)
        else:
            o_ref[row] = sums[row]


def spread_tile(padded, taps, *extra):
    rows, cols, channels = padded.shape
    tile_rows, tile_cols = rows - KSIZE + 1, cols - KSIZE + 1
    tile = pl.BlockSpec((tile_rows, tile_cols, LANES), lambda i: (0, 0, i))
    more = [tile, pl.BlockSpec((tile_rows, LANES), lambda i: (0, 0))] if extra else []
    return pl.pallas_call(
        spread_kernel,
        grid=(channels // LANES,),
        in_specs=[
            pl.BlockSpec((rows, cols, LANES), lambda i: (0, 0, i)),
            pl.BlockSpec((KSIZE * KSIZE, LANES), lambda i: (0, i)),
        ]
        + more,
        out_specs=tile,
        out_shape=jax.ShapeDtypeStruct(
            (tile_rows, tile_cols, channels), jnp.bfloat16 if extra else jnp.float32
        ),
        cost_estimate=pl.CostEstimate(
            flops=8 * KSIZE * KSIZE * tile_rows * tile_cols * channels,
            bytes_accessed=4 * rows * cols * channels,
            transcendentals=0,
        ),
    )(padded.astype(jnp.float32), taps, *extra)


def sums_kernel(x_ref, g_ref, o_ref):
    micro_count, tile_rows, tile_cols = g_ref.shape[:3]
    for row_tap in range(KSIZE):
        for col_tap in range(KSIZE):
            folded = None
            for chart in range(micro_count):
                for row in range(tile_rows):
                    window = x_ref[chart, row + row_tap, col_tap : col_tap + tile_cols, :]
                    term = window * g_ref[chart, row]
                    folded = term if folded is None else folded + term
            tap = row_tap * KSIZE + col_tap
            o_ref[tap : tap + 1, :] = jnp.sum(folded, axis=0, keepdims=True)


def kernel_sums(padded, grads):
    micro_count, rows, cols, channels = padded.shape
    tile_rows, tile_cols = grads.shape[1:3]
    return pl.pallas_call(
        sums_kernel,
        grid=(channels // LANES,),
        in_specs=[
            pl.BlockSpec((micro_count, rows, cols, LANES), lambda i: (0, 0, 0, i)),
            pl.BlockSpec((micro_count, tile_rows, tile_cols, LANES), lambda i: (0, 0, 0, i)),
        ],
        out_specs=pl.BlockSpec((KSIZE * KSIZE, LANES), lambda i: (0, i)),
        out_shape=jax.ShapeDtypeStruct((KSIZE * KSIZE, channels), jnp.float32),
        cost_estimate=pl.CostEstimate(
            flops=8 * KSIZE * KSIZE * micro_count * tile_rows * tile_cols * channels,
            bytes_accessed=4 * micro_count * rows * cols * channels,
            transcendentals=0,
        ),
    )(padded.astype(jnp.float32), grads.astype(jnp.float32))


def norm_stats(mixed):
    centred = mixed - jnp.mean(mixed, axis=-1, keepdims=True)
    inv_sigma = lax.rsqrt(jnp.mean(centred * centred, axis=-1, keepdims=True) + eps)
    return (centred * inv_sigma, inv_sigma)


def contract_rows(former, latter):
    return lax.dot_general(
        former, latter, (((0,), (0,)), ((), ())), preferred_element_type=jnp.float32
    )


def contract_cols(former, latter):
    return lax.dot_general(
        former, latter, (((1,), (1,)), ((), ())), preferred_element_type=jnp.float32
    )


def chip_pairs(low, high, step):
    return [(2 * z + core, 2 * (z + step) + core) for z in range(low, high) for core in range(2)]


def swap_cores(value):
    count = lax.axis_size("dp")
    pairs = [(i, i + 1 - 2 * (i % 2)) for i in range(count)]
    return lax.ppermute(value, "dp", pairs)


def gather_step(right, left, hop):
    chips = lax.axis_size("dp") // 2
    return (
        lax.ppermute(right, "dp", chip_pairs(hop - 1, chips - 1, 1)),
        lax.ppermute(left, "dp", chip_pairs(1, chips - hop + 1, -1)),
    )


def gather_join(shard, hops):
    chips = lax.axis_size("dp") // 2
    line = [right for right, _ in hops[::-1]] + [shard] + [left for _, left in hops]
    place = lax.axis_index("dp") // 2
    return lax.dynamic_slice_in_dim(jnp.stack(line), chips - 1 - place, chips, 0)


def gather_line(shard):
    hops = []
    for hop in range(1, lax.axis_size("dp") // 2):
        hops.append(gather_step(*(hops[-1] if hops else (shard, shard)), hop))
    return gather_join(shard, hops)


def gather_cores(part):
    other = swap_cores(part)
    first = lax.rem(lax.axis_index("dp"), 2) == 0
    low = jnp.where(first, part, other)
    high = jnp.where(first, other, part)
    return jnp.stack([low, high], axis=1).reshape(-1, part.shape[-1])


def scatter_cores(total):
    count = lax.axis_size("dp")
    split = total.astype(jnp.bfloat16)
    split = split.reshape(count // 2, 2, total.shape[0] // count, total.shape[1])
    core = lax.rem(lax.axis_index("dp"), 2)
    away = lax.dynamic_index_in_dim(split, 1 - core, 1, keepdims=False)
    mine = lax.dynamic_index_in_dim(split, core, 1, keepdims=False)
    both = mine.astype(jnp.float32) + swap_cores(away).astype(jnp.float32)
    return both.astype(jnp.bfloat16)


def scatter_chips(pair_sum):
    chips = pair_sum.shape[0]
    place = lax.axis_index("dp") // 2

    def term(index, held):
        block = lax.dynamic_index_in_dim(
            pair_sum, jnp.clip(index, 0, chips - 1), 0, keepdims=False
        )
        return block if held is None else sum_two(block, held).astype(jnp.bfloat16)

    right, left = None, None
    for hop in range(1, chips):
        away = chips - hop
        right = lax.ppermute(
            term(place + away, right), "dp", chip_pairs(0, min(hop, chips - 1), 1)
        )
        left = lax.ppermute(term(place - away, left), "dp", chip_pairs(max(away, 1), chips, -1))
    total = sum_two(term(place, None), right)
    return total if left is None else sum_two(total, left)


def sum_two(former, latter):
    return former.astype(jnp.float32) + latter.astype(jnp.float32)


def sum_small(value):
    count = lax.axis_size("dp")
    if count & (count - 1):
        return lax.psum(value, "dp")
    reach = 1
    while reach < count:
        pairs = [(i, i ^ reach) for i in range(count)]
        value = value + lax.ppermute(value, "dp", pairs)
        reach *= 2
    return value


def per_device(
    block_inputs,
    top_grad,
    depth_kernel,
    norm_gain,
    layer_scale,
    expand_weight,
    reduce_weight,
    chart_rows,
):
    segment_count = lax.axis_size("segment")
    group_count = lax.axis_size("dp")
    segment_index = lax.axis_index("segment")
    group_index = lax.axis_index("dp")
    micro_count, tile_rows, tile_cols, channels = block_inputs.shape[1:]
    hidden_width = expand_weight.shape[2]
    half_width = KSIZE // 2
    tokens = tile_rows * tile_cols
    kernel = depth_kernel[0]
    flipped = kernel[::-1, ::-1]
    gain_row = norm_gain[0]
    scale_row = layer_scale[0]
    row_ids = group_index * tile_rows + jnp.arange(tile_rows, dtype=jnp.int32)
    row_keep = (row_ids[None, :] < chart_rows[:, None]).astype(jnp.float32)
    masked = (block_inputs[0].astype(jnp.float32) * row_keep[:, :, None, None]).astype(jnp.bfloat16)
    rimmed = extended(masked, (("dp", 1),), half_width)
    rimmed = jnp.pad(rimmed, ((0, 0), (0, 0), (half_width, half_width), (0, 0)))
    reduce_full = lax.all_gather(reduce_weight[0], "dp", axis=0, tiled=True)
    expand_full = gather_cores(gather_line(expand_weight[0]))

    taps_forward = kernel.reshape(-1, channels)
    taps_back = flipped.reshape(-1, channels)
    mixed = jnp.stack([spread_tile(rimmed[m], taps_forward) for m in range(micro_count)])
    normal_z, inv_sigma = norm_stats(mixed.reshape(micro_count, tokens, channels))
    normed = (normal_z * gain_row).astype(jnp.bfloat16).reshape(-1, channels)
    pre_act = jnp.dot(normed, expand_full, preferred_element_type=jnp.float32)
    hidden = gelu_value(pre_act).astype(jnp.bfloat16)
    slope = gelu_slope(pre_act).reshape(micro_count, tokens, hidden_width)

    def pick(array, slot):
        return lax.dynamic_index_in_dim(array, slot, 0, keepdims=False)

    def put(array, value, slot):
        return lax.dynamic_update_index_in_dim(array, value, slot, 0)

    incoming = jnp.zeros((tokens, channels), jnp.bfloat16)
    tops = top_grad.reshape(micro_count, tokens, channels)
    token_keep = jnp.repeat(row_keep, tile_cols, axis=1)[:, :, None]
    out_grads = jnp.zeros((micro_count, tokens, channels), jnp.bfloat16)
    pre_grads = jnp.zeros((micro_count, tokens, hidden_width), jnp.bfloat16)
    mixed_grads = jnp.zeros((micro_count, tokens, channels), jnp.bfloat16)
    normed_grads = jnp.zeros((micro_count, tokens, channels), jnp.float32)
    results = jnp.zeros((micro_count, tokens, channels), jnp.bfloat16)
    ticks = segment_count + micro_count - 1
    for tick_id in range(ticks):
        slot = jnp.clip(tick_id - (segment_count - 1 - segment_index), 0, micro_count - 1)
        arriving = jnp.where(segment_index == segment_count - 1, pick(tops, slot), incoming)
        keep = pick(token_keep, slot)
        out_grad = (arriving.astype(jnp.float32) * keep).astype(jnp.bfloat16)
        out_grads = put(out_grads, out_grad, slot)
        if tick_id == ticks - 1:
            flat_out = out_grads.reshape(-1, channels)
            hidden_total = contract_rows(hidden, flat_out).astype(jnp.bfloat16)
            hidden_total, out_grad = lax.optimization_barrier((hidden_total, out_grad))
            hidden_sum = lax.psum_scatter(
                hidden_total, "dp", scatter_dimension=0, tiled=True
            ).astype(jnp.float32)
        scaled_grad = (out_grad.astype(jnp.float32) * scale_row).astype(jnp.bfloat16)
        hidden_grad = contract_cols(scaled_grad, reduce_full)
        pre_grad = (hidden_grad * pick(slope, slot)).astype(jnp.bfloat16)
        pre_grads = put(pre_grads, pre_grad, slot)
        if tick_id == ticks - 1:
            input_total = contract_rows(normed, pre_grads.reshape(-1, hidden_width))
            input_total, pre_grad = lax.optimization_barrier(
                (input_total.astype(jnp.bfloat16), pre_grad)
            )
            input_sum = scatter_chips(scatter_cores(input_total))
        normed_grad = contract_cols(pre_grad, expand_full)
        normed_grads = put(normed_grads, normed_grad, slot)
        zed = pick(normal_z, slot)
        scaled_u = normed_grad * gain_row
        mixed_grad = (
            pick(inv_sigma, slot)
            * (
                scaled_u
                - jnp.mean(scaled_u, axis=-1, keepdims=True)
                - zed * jnp.mean(scaled_u * zed, axis=-1, keepdims=True)
            )
        ).astype(jnp.bfloat16)
        mixed_grads = put(mixed_grads, mixed_grad, slot)
        mixed_tile = mixed_grad.reshape(tile_rows, tile_cols, channels)
        grad_rimmed = extended(mixed_tile, (("dp", 0),), half_width)
        grad_padded = jnp.pad(grad_rimmed, ((0, 0), (half_width, half_width), (0, 0)))
        line_keep = jnp.broadcast_to(pick(row_keep, slot)[:, None], (tile_rows, LANES))
        input_grad = spread_tile(
            grad_padded, taps_back, arriving.reshape(tile_rows, tile_cols, channels), line_keep
        ).reshape(tokens, channels)
        results = put(results, input_grad, slot)
        if tick_id < ticks - 1:
            incoming = from_behind(input_grad, "segment", -1)
    kernel_part = kernel_sums(
        rimmed, mixed_grads.reshape(micro_count, tile_rows, tile_cols, channels)
    )
    gain_part = jnp.sum(normed_grads * normal_z, axis=(0, 1))
    branch = jnp.dot(hidden, reduce_full, preferred_element_type=jnp.float32)
    scale_part = jnp.sum(flat_out.astype(jnp.float32) * branch, axis=0)
    small = jnp.concatenate([kernel_part, gain_part[None], scale_part[None]], axis=0)
    small = sum_small(small)
    taps = KSIZE * KSIZE
    grad_norm = 1.0 / math.sqrt(micro_count * tokens * group_count)
    small = small * grad_norm
    return (
        results.reshape((1,) + block_inputs.shape[1:]),
        (input_sum * grad_norm)[None],
        (hidden_sum * scale_row * grad_norm)[None],
        small[:taps].reshape(1, KSIZE, KSIZE, channels),
        small[taps][None],
        small[taps + 1][None],
    )


def solution(mesh):
    placed = (
        P("segment", None, "dp", None, None),
        P(None, "dp", None, None),
        P("segment", None, None, None),
        P("segment", None),
        P("segment", None),
        P("segment", "dp", None),
        P("segment", "dp", None),
        P(),
    )
    return jax.shard_map(
        per_device,
        mesh=mesh,
        in_specs=placed,
        out_specs=(
            P("segment", None, "dp", None, None),
            P("segment", "dp", None),
            P("segment", "dp", None),
            P("segment", None, None, None),
            P("segment", None),
            P("segment", None),
        ),
        check_vma=False,
    )
```

```python
import math

import jax
import jax.numpy as jnp
from jax import lax
from jax.experimental import pallas as pl
from jax.sharding import PartitionSpec as P

KSIZE = 7


root_half = 0.7071067811865476
inv_root_tau = 0.3989422804014327
eps = 1e-06


def extended(block, sides, width):
    for axis, dim in sides:
        count = lax.axis_size(axis)
        forward = [(i, i + 1) for i in range(count - 1)]
        backward = [(target, source) for source, target in forward]
        low = lax.ppermute(
            lax.slice_in_dim(block, block.shape[dim] - width, None, axis=dim), axis, forward
        )
        high = lax.ppermute(lax.slice_in_dim(block, 0, width, axis=dim), axis, backward)
        block = jnp.concatenate([low, block, high], axis=dim)
    return block


def from_behind(value, axis, by):
    length = lax.axis_size(axis)
    pairs = [(i, i + by) for i in range(length) if 0 <= i + by < length]
    return lax.ppermute(value, axis, pairs)


def gelu_value(pre_act):
    return 0.5 * pre_act * (1.0 + lax.erf(pre_act * root_half))


def gelu_slope(pre_act):
    return (
        0.5 * (1.0 + lax.erf(pre_act * root_half))
        + pre_act * jnp.exp(-0.5 * pre_act * pre_act) * inv_root_tau
    )


LANES = 128


def spread_kernel(x_ref, k_ref, *rest):
    o_ref = rest[-1]
    tile_rows, tile_cols = o_ref.shape[:2]
    sums = [None] * tile_rows
    for line in range(tile_rows + KSIZE - 1):
        for col_tap in range(KSIZE):
            window = x_ref[line, col_tap : col_tap + tile_cols, :]
            for row in range(tile_rows):
                row_tap = line - row
                if 0 <= row_tap < KSIZE:
                    tap = row_tap * KSIZE + col_tap
                    term = k_ref[tap : tap + 1, :] * window
                    sums[row] = term if sums[row] is None else sums[row] + term
    for row in range(tile_rows):
        if len(rest) > 1:
            held = rest[0][row].astype(jnp.float32) + rest[1][row : row + 1, :] * sums[row]
            o_ref[row] = held.astype(jnp.bfloat16)
        else:
            o_ref[row] = sums[row]


def spread_tile(padded, taps, *extra):
    rows, cols, channels = padded.shape
    tile_rows, tile_cols = rows - KSIZE + 1, cols - KSIZE + 1
    tile = pl.BlockSpec((tile_rows, tile_cols, LANES), lambda i: (0, 0, i))
    more = [tile, pl.BlockSpec((tile_rows, LANES), lambda i: (0, 0))] if extra else []
    return pl.pallas_call(
        spread_kernel,
        grid=(channels // LANES,),
        in_specs=[
            pl.BlockSpec((rows, cols, LANES), lambda i: (0, 0, i)),
            pl.BlockSpec((KSIZE * KSIZE, LANES), lambda i: (0, i)),
        ]
        + more,
        out_specs=tile,
        out_shape=jax.ShapeDtypeStruct(
            (tile_rows, tile_cols, channels), jnp.bfloat16 if extra else jnp.float32
        ),
        cost_estimate=pl.CostEstimate(
            flops=8 * KSIZE * KSIZE * tile_rows * tile_cols * channels,
            bytes_accessed=4 * rows * cols * channels,
            transcendentals=0,
        ),
    )(padded.astype(jnp.float32), taps, *extra)


def sums_kernel(x_ref, g_ref, o_ref):
    micro_count, tile_rows, tile_cols = g_ref.shape[:3]
    for row_tap in range(KSIZE):
        for col_tap in range(KSIZE):
            folded = None
            for chart in range(micro_count):
                for row in range(tile_rows):
                    window = x_ref[chart, row + row_tap, col_tap : col_tap + tile_cols, :]
                    term = window * g_ref[chart, row]
                    folded = term if folded is None else folded + term
            tap = row_tap * KSIZE + col_tap
            o_ref[tap : tap + 1, :] = jnp.sum(folded, axis=0, keepdims=True)


def kernel_sums(padded, grads):
    micro_count, rows, cols, channels = padded.shape
    tile_rows, tile_cols = grads.shape[1:3]
    return pl.pallas_call(
        sums_kernel,
        grid=(channels // LANES,),
        in_specs=[
            pl.BlockSpec((micro_count, rows, cols, LANES), lambda i: (0, 0, 0, i)),
            pl.BlockSpec((micro_count, tile_rows, tile_cols, LANES), lambda i: (0, 0, 0, i)),
        ],
        out_specs=pl.BlockSpec((KSIZE * KSIZE, LANES), lambda i: (0, i)),
        out_shape=jax.ShapeDtypeStruct((KSIZE * KSIZE, channels), jnp.float32),
        cost_estimate=pl.CostEstimate(
            flops=8 * KSIZE * KSIZE * micro_count * tile_rows * tile_cols * channels,
            bytes_accessed=4 * micro_count * rows * cols * channels,
            transcendentals=0,
        ),
    )(padded.astype(jnp.float32), grads.astype(jnp.float32))


def norm_stats(mixed):
    centred = mixed - jnp.mean(mixed, axis=-1, keepdims=True)
    inv_sigma = lax.rsqrt(jnp.mean(centred * centred, axis=-1, keepdims=True) + eps)
    return (centred * inv_sigma, inv_sigma)


def contract_rows(former, latter):
    return lax.dot_general(
        former, latter, (((0,), (0,)), ((), ())), preferred_element_type=jnp.float32
    )


def contract_cols(former, latter):
    return lax.dot_general(
        former, latter, (((1,), (1,)), ((), ())), preferred_element_type=jnp.float32
    )


def chip_pairs(low, high, step):
    return [(2 * z + core, 2 * (z + step) + core) for z in range(low, high) for core in range(2)]


def swap_cores(value):
    count = lax.axis_size("dp")
    pairs = [(i, i + 1 - 2 * (i % 2)) for i in range(count)]
    return lax.ppermute(value, "dp", pairs)


def gather_step(right, left, hop):
    chips = lax.axis_size("dp") // 2
    return (
        lax.ppermute(right, "dp", chip_pairs(hop - 1, chips - 1, 1)),
        lax.ppermute(left, "dp", chip_pairs(1, chips - hop + 1, -1)),
    )


def gather_join(shard, hops):
    chips = lax.axis_size("dp") // 2
    line = [right for right, _ in hops[::-1]] + [shard] + [left for _, left in hops]
    place = lax.axis_index("dp") // 2
    return lax.dynamic_slice_in_dim(jnp.stack(line), chips - 1 - place, chips, 0)


def gather_two(first, second):
    chips = lax.axis_size("dp") // 2
    early, late = [], []
    for hop in range(1, chips + 1):
        if hop > 1:
            ahead = late[-1] if late else (second, second)
            if hop == 2:
                second = lax.optimization_barrier((second,) + early[0])[0]
                ahead = (second, second)
            late.append(gather_step(*ahead, hop - 1))
        if hop < chips:
            early.append(gather_step(*(early[-1] if early else (first, first)), hop))
    return gather_join(first, early), gather_join(second, late)


def gather_cores(part):
    other = swap_cores(part)
    first = lax.rem(lax.axis_index("dp"), 2) == 0
    low = jnp.where(first, part, other)
    high = jnp.where(first, other, part)
    return jnp.stack([low, high], axis=1).reshape(-1, part.shape[-1])


def sum_small(value):
    count = lax.axis_size("dp")
    if count & (count - 1):
        return lax.psum(value, "dp")
    reach = 1
    while reach < count:
        pairs = [(i, i ^ reach) for i in range(count)]
        value = value + lax.ppermute(value, "dp", pairs)
        reach *= 2
    return value


def per_device(
    block_inputs,
    top_grad,
    depth_kernel,
    norm_gain,
    layer_scale,
    expand_weight,
    reduce_weight,
    chart_rows,
):
    segment_count = lax.axis_size("segment")
    group_count = lax.axis_size("dp")
    segment_index = lax.axis_index("segment")
    group_index = lax.axis_index("dp")
    micro_count, tile_rows, tile_cols, channels = block_inputs.shape[1:]
    hidden_width = expand_weight.shape[2]
    half_width = KSIZE // 2
    tokens = tile_rows * tile_cols
    kernel = depth_kernel[0]
    flipped = kernel[::-1, ::-1]
    gain_row = norm_gain[0]
    scale_row = layer_scale[0]
    row_ids = group_index * tile_rows + jnp.arange(tile_rows, dtype=jnp.int32)
    row_keep = (row_ids[None, :] < chart_rows[:, None]).astype(jnp.float32)
    masked = (block_inputs[0].astype(jnp.float32) * row_keep[:, :, None, None]).astype(jnp.bfloat16)
    rimmed = extended(masked, (("dp", 1),), half_width)
    rimmed = jnp.pad(rimmed, ((0, 0), (0, 0), (half_width, half_width), (0, 0)))
    expand_part, reduce_part = gather_two(expand_weight[0], reduce_weight[0])
    expand_full = gather_cores(expand_part)

    taps_forward = kernel.reshape(-1, channels)
    taps_back = flipped.reshape(-1, channels)
    mixed = jnp.stack([spread_tile(rimmed[m], taps_forward) for m in range(micro_count)])
    normal_z, inv_sigma = norm_stats(mixed.reshape(micro_count, tokens, channels))
    normed = (normal_z * gain_row).astype(jnp.bfloat16).reshape(-1, channels)
    pre_act = jnp.dot(normed, expand_full, preferred_element_type=jnp.float32)
    hidden = gelu_value(pre_act).astype(jnp.bfloat16)
    slope = gelu_slope(pre_act).reshape(micro_count, tokens, hidden_width)
    reduce_full = gather_cores(reduce_part)

    def pick(array, slot):
        return lax.dynamic_index_in_dim(array, slot, 0, keepdims=False)

    def put(array, value, slot):
        return lax.dynamic_update_index_in_dim(array, value, slot, 0)

    incoming = jnp.zeros((tokens, channels), jnp.bfloat16)
    tops = top_grad.reshape(micro_count, tokens, channels)
    token_keep = jnp.repeat(row_keep, tile_cols, axis=1)[:, :, None]
    out_grads = jnp.zeros((micro_count, tokens, channels), jnp.bfloat16)
    pre_grads = jnp.zeros((micro_count, tokens, hidden_width), jnp.bfloat16)
    mixed_grads = jnp.zeros((micro_count, tokens, channels), jnp.bfloat16)
    normed_grads = jnp.zeros((micro_count, tokens, channels), jnp.float32)
    results = jnp.zeros((micro_count, tokens, channels), jnp.bfloat16)
    ticks = segment_count + micro_count - 1
    for tick_id in range(ticks):
        slot = jnp.clip(tick_id - (segment_count - 1 - segment_index), 0, micro_count - 1)
        arriving = jnp.where(segment_index == segment_count - 1, pick(tops, slot), incoming)
        keep = pick(token_keep, slot)
        out_grad = (arriving.astype(jnp.float32) * keep).astype(jnp.bfloat16)
        out_grads = put(out_grads, out_grad, slot)
        if tick_id == ticks - 1:
            flat_out = out_grads.reshape(-1, channels)
            hidden_total = contract_rows(hidden, flat_out).astype(jnp.bfloat16)
            hidden_total, out_grad = lax.optimization_barrier((hidden_total, out_grad))
            hidden_sum = lax.psum_scatter(
                hidden_total, "dp", scatter_dimension=0, tiled=True
            ).astype(jnp.float32)
        scaled_grad = (out_grad.astype(jnp.float32) * scale_row).astype(jnp.bfloat16)
        hidden_grad = contract_cols(scaled_grad, reduce_full)
        pre_grad = (hidden_grad * pick(slope, slot)).astype(jnp.bfloat16)
        pre_grads = put(pre_grads, pre_grad, slot)
        if tick_id == ticks - 1:
            input_total = contract_rows(normed, pre_grads.reshape(-1, hidden_width))
            input_total, pre_grad = lax.optimization_barrier(
                (input_total.astype(jnp.bfloat16), pre_grad)
            )
            input_sum = lax.psum_scatter(
                input_total, "dp", scatter_dimension=0, tiled=True
            ).astype(jnp.float32)
        normed_grad = contract_cols(pre_grad, expand_full)
        normed_grads = put(normed_grads, normed_grad, slot)
        zed = pick(normal_z, slot)
        scaled_u = normed_grad * gain_row
        mixed_grad = (
            pick(inv_sigma, slot)
            * (
                scaled_u
                - jnp.mean(scaled_u, axis=-1, keepdims=True)
                - zed * jnp.mean(scaled_u * zed, axis=-1, keepdims=True)
            )
        ).astype(jnp.bfloat16)
        mixed_grads = put(mixed_grads, mixed_grad, slot)
        mixed_tile = mixed_grad.reshape(tile_rows, tile_cols, channels)
        grad_rimmed = extended(mixed_tile, (("dp", 0),), half_width)
        grad_padded = jnp.pad(grad_rimmed, ((0, 0), (half_width, half_width), (0, 0)))
        line_keep = jnp.broadcast_to(pick(row_keep, slot)[:, None], (tile_rows, LANES))
        input_grad = spread_tile(
            grad_padded, taps_back, arriving.reshape(tile_rows, tile_cols, channels), line_keep
        ).reshape(tokens, channels)
        results = put(results, input_grad, slot)
        if tick_id < ticks - 1:
            incoming = from_behind(input_grad, "segment", -1)
    kernel_part = kernel_sums(
        rimmed, mixed_grads.reshape(micro_count, tile_rows, tile_cols, channels)
    )
    gain_part = jnp.sum(normed_grads * normal_z, axis=(0, 1))
    branch = jnp.dot(hidden, reduce_full, preferred_element_type=jnp.float32)
    scale_part = jnp.sum(flat_out.astype(jnp.float32) * branch, axis=0)
    small = jnp.concatenate([kernel_part, gain_part[None], scale_part[None]], axis=0)
    small = sum_small(small)
    taps = KSIZE * KSIZE
    grad_norm = 1.0 / math.sqrt(micro_count * tokens * group_count)
    small = small * grad_norm
    return (
        results.reshape((1,) + block_inputs.shape[1:]),
        (input_sum * grad_norm)[None],
        (hidden_sum * scale_row * grad_norm)[None],
        small[:taps].reshape(1, KSIZE, KSIZE, channels),
        small[taps][None],
        small[taps + 1][None],
    )


def solution(mesh):
    placed = (
        P("segment", None, "dp", None, None),
        P(None, "dp", None, None),
        P("segment", None, None, None),
        P("segment", None),
        P("segment", None),
        P("segment", "dp", None),
        P("segment", "dp", None),
        P(),
    )
    return jax.shard_map(
        per_device,
        mesh=mesh,
        in_specs=placed,
        out_specs=(
            P("segment", None, "dp", None, None),
            P("segment", "dp", None),
            P("segment", "dp", None),
            P("segment", None, None, None),
            P("segment", None),
            P("segment", None),
        ),
        check_vma=False,
    )
```
